256 devices in a mesh: order: 16 (over z_lo, x), lat: 16 (over y, z_hi, core).
Axes of the slice: x: 4, y: 4, z: 8 (z_hi: 2, z_lo: 4; z = z_hi * 4 + z_lo), core: 2. Of those that a mesh axis runs over, the one named last changes fastest.
Arguments:
- coeffs: bfloat16 [1536, 32, 32, 274], P('order', 'lat'), may hold values from -6 to 6
- coupling: bfloat16 [4, 1536, 32, 32, 64], P(None, 'order', 'lat'), may hold values from -0.75 to 0.75
- pattern: int32 [4, 1536, 32], P(None, 'order', 'lat'), may hold values from 0 to 1
- assign: int32 [1536], replicated, may hold values from 0 to 1535, as said below
Outputs:
- spectral: bfloat16 [1536, 32, 32, 274], P('order', 'lat')
The draws below stay inside these ranges and needn't reach their ends.
Inputs may be any that keep to these rules, and one draw needn't show every extreme that they name: `assign`: each of the 1536 orders appears exactly once. Entries k * 96 + c * 6 + j, for j below 6, hold orders from c * 96 to (c + 1) * 96 - 1.
All inputs are finite; a program needn't handle non-finite values.
Results may differ from the reference program's by a relative error of at most 0.0064.
Values may be sent and summed in bfloat16 or wider, within the bound.
No kernel may reach another device: no remote copies, remote signals or barrier semaphores. Data moves between devices by JAX's collectives and lax.ppermute only.
A program may use at most 128 MiB of HBM per device.

```python
import jax
import jax.numpy as jnp
from jax import lax

K = 32
C = 274
ORD_DEV = 96
BOX = 2
LEVELS = 4
M = 1536
NBOX = 32
N_ORDER = 16
N_LAT = 16


def draw_assign(key, part):
    key = jax.random.fold_in(key, 7)
    keys = jax.random.split(key, N_ORDER)
    shuffled = jax.vmap(lambda one_key: jax.random.permutation(one_key, ORD_DEV))(keys)
    shuffled = shuffled.astype(jnp.int32) + (jnp.arange(N_ORDER, dtype=jnp.int32) * ORD_DEV)[:, None]
    grouped = shuffled.reshape(N_ORDER, N_ORDER, ORD_DEV // N_ORDER)
    return jnp.transpose(grouped, (1, 0, 2)).reshape(N_ORDER * ORD_DEV).astype(jnp.int32)


def place_ends(values, rng, smallest, top_value):
    dims = values.shape
    index_at = [jax.random.randint(jax.random.fold_in(rng, axis), (), 0, dims[axis]) for axis in range(len(dims))]
    values = values.at[tuple(index_at)].set(smallest)
    longest = dims.index(max(dims))
    index_at[longest] = (index_at[longest] + 1) % dims[longest]
    return values.at[tuple(index_at)].set(top_value)


def block_scale(key, extent, shards, least, largest):
    loudness = 1.0
    for position, parts in shards:
        draws = jax.random.uniform(jax.random.fold_in(jax.random.fold_in(key, 6), position), (parts,), jnp.float32, least / len(shards), largest / len(shards))
        loudness = loudness * jnp.repeat(jnp.exp(draws), extent[position] // parts).reshape((-1,) + (1,) * (len(extent) - 1 - position))
    return loudness


def centred(own_key, shape, deviation, limit, cuts=(), held_as=jnp.bfloat16):
    entries = deviation * jax.random.normal(own_key, shape, jnp.float32)
    if cuts:
        entries = entries * block_scale(own_key, shape, cuts, -0.22, 0.18)
    return jnp.clip(entries, -limit, limit).astype(held_as)


def setup_inputs(seed: int = 0) -> dict:
    streams_of = jax.random.split(jax.random.key(seed), 5)
    return {
        "coeffs": centred(streams_of[0], (M, NBOX, K, C), 1.0, 6.0, ((0, 16), (1, 16))),
        "coupling": centred(streams_of[1], (LEVELS, M, NBOX, K, 2 * K), (2 * K) ** -0.5, 0.75, ((1, 16), (2, 16))),
        "pattern": place_ends(jax.random.randint(streams_of[2], (LEVELS, M, NBOX), 0, BOX), jax.random.fold_in(streams_of[2], 1), 0, BOX - 1).astype(jnp.int32),
        "assign": draw_assign(jax.random.fold_in(streams_of[4], 71), 0),
    }


def reference(coeffs, coupling, pattern, assign):
    log_lat = N_LAT.bit_length() - 1
    box_ids = jnp.arange(NBOX, dtype=jnp.int32)
    owners = box_ids // BOX

    def one_order(order_idx):
        blocks = lax.dynamic_index_in_dim(coeffs, order_idx, 0, keepdims=False)
        weights = lax.dynamic_index_in_dim(coupling, order_idx, 1, keepdims=False)
        selectors = lax.dynamic_index_in_dim(pattern, order_idx, 1, keepdims=False)
        for level_idx in range(LEVELS):
            flip_bit = 1 << (level_idx % log_lat)
            source = ((owners ^ flip_bit) * BOX + selectors[level_idx]).astype(jnp.int32)
            partner = jnp.take(blocks, source, axis=0)
            stacked = jnp.concatenate([blocks, partner], axis=1).astype(jnp.float32)
            new_blocks = jnp.einsum("gij,gjc->gic", weights[level_idx].astype(jnp.float32), stacked)
            blocks = new_blocks.astype(jnp.bfloat16)
        return blocks

    result = lax.map(one_order, jnp.arange(M, dtype=jnp.int32))
    inverse = jnp.zeros((M,), jnp.int32).at[assign].set(jnp.arange(M, dtype=jnp.int32))
    return jnp.take(result, inverse, axis=0)
```

```python
import functools

import jax
import jax.numpy as jnp
from jax import lax
from jax.experimental import pallas as pl
from jax.experimental.pallas import tpu as pltpu
from jax.sharding import PartitionSpec as P

LEVELS = 4
LANES = 128


def from_partner(value, bit):
    size = lax.axis_size("lat")
    return lax.ppermute(value, "lat", [(i, i ^ 1 << bit) for i in range(size)])


def level_kernel(spec, lev, tail_w, pat_ref, w_ref, *refs):
    n_in = spec["n_in"]
    own, far, outs = refs[:n_in], refs[n_in : 2 * n_in], refs[2 * n_in :]
    groups, per_peer = w_ref.shape[0], w_ref.shape[1]
    boxes = w_ref.shape[2]
    lane = lax.broadcasted_iota(jnp.int32, (w_ref.shape[3], LANES), 1)
    base = pl.program_id(0) * groups
    total = pl.num_programs(0) * groups * per_peer

    def group(c, carry):
        for out, slots in zip(outs, spec["slots"]):
            for at, slot in enumerate(slots):
                for g in range(boxes):

                    def product(order, src, idx):
                        sel = pat_ref[(lev * total + (base + c) * per_peer + order) * boxes + g]
                        rhs = jnp.concatenate([own[src][c, idx, g], far[src][c, idx, sel]], axis=0)
                        return jnp.dot(w_ref[c, order, g], rhs, preferred_element_type=jnp.float32)

                    if slot[0] == "m":
                        acc = product(slot[3], slot[1], slot[2])
                    else:
                        acc = product(0, slot[1], slot[2])
                        for j in range(1, per_peer):
                            acc = jnp.where(lane < j * tail_w, acc, product(j, slot[1], slot[2]))
                    out[c, at, g] = acc.astype(jnp.bfloat16)
        return carry

    lax.fori_loop(0, groups, group, 0)


def run_level(lev, tail_w, slots, pattern, weights, own, far, steps=4):
    peers, per_peer, boxes, rank, _ = weights.shape
    step = peers // steps
    spec = {"n_in": len(own), "slots": slots}
    blk = lambda shape: pl.BlockSpec((step,) + tuple(shape[1:]), lambda i, p: (i,) + (0,) * (len(shape) - 1))
    out_shapes = [jax.ShapeDtypeStruct((peers, len(s), boxes, rank, LANES), jnp.bfloat16) for s in slots]
    dots = sum(sum(1 if x[0] == "m" else per_peer for x in s) for s in slots) * peers * boxes
    moved = sum(a.size for a in (*own, *far, weights)) * 2 + sum(o.size for o in out_shapes) * 2
    return pl.pallas_call(
        functools.partial(level_kernel, spec, lev, tail_w),
        grid_spec=pltpu.PrefetchScalarGridSpec(
            num_scalar_prefetch=1,
            grid=(steps,),
            in_specs=[blk(weights.shape)] + [blk(a.shape) for a in (*own, *far)],
            out_specs=[blk(o.shape) for o in out_shapes],
        ),
        out_shape=out_shapes,
        cost_estimate=pl.CostEstimate(
            flops=dots * 2 * rank * 2 * rank * LANES, bytes_accessed=moved, transcendentals=0
        ),
    )(pattern, weights, *own, *far)


def place_kernel(tail_w, n_main, me_ref, assign_ref, *refs):
    ins, out_ref = refs[:-1], refs[-1]
    peers = ins[0].shape[0]
    per_peer = n_main
    boxes, rank = ins[0].shape[2], ins[0].shape[3]
    local = peers * per_peer
    me = me_ref[0]
    half = per_peer // 2

    def peer(k, carry):
        for j in range(per_peer):
            to = assign_ref[k * local + me * per_peer + j] - me * local
            for g in range(boxes):
                a = ins[j // half][k, j % half, g]
                b = ins[2][k, 1 + j, g] if j < half else ins[3][k, j - half, g]
                t = ins[2][k, 0, g].astype(jnp.float32)
                if j:
                    t = pltpu.roll(t, LANES - j * tail_w, 1)
                out_ref[to, g, :, 0:LANES] = a
                out_ref[to, g, :, LANES : 2 * LANES] = b
                out_ref[to, g, :, 2 * LANES : 2 * LANES + tail_w] = t[:, :tail_w].astype(jnp.bfloat16)
        return carry

    lax.fori_loop(0, peers, peer, 0)


def place(tail_w, me, assign, parts, cols):
    peers, _, boxes, rank, _ = parts[0].shape
    per_peer = parts[0].shape[1] * 2
    local = peers * per_peer
    vmem = pl.BlockSpec(memory_space=pltpu.VMEM)
    smem = pl.BlockSpec(memory_space=pltpu.SMEM)
    return pl.pallas_call(
        functools.partial(place_kernel, tail_w, per_peer),
        in_specs=[smem, smem] + [vmem] * len(parts),
        out_specs=vmem,
        out_shape=jax.ShapeDtypeStruct((local, boxes, rank, cols), jnp.bfloat16),
        compiler_params=pltpu.CompilerParams(vmem_limit_bytes=32 << 20),
        cost_estimate=pl.CostEstimate(
            flops=0, bytes_accessed=4 * local * boxes * rank * cols, transcendentals=0
        ),
    )(me, assign, *parts)


def per_device(coeffs, coupling, pattern, assign):
    local, boxes, rank, cols = coeffs.shape
    peers = lax.axis_size("order")
    per_peer = local // peers
    half = per_peer // 2
    tail_w = cols - 2 * LANES
    flat_pattern = pattern.reshape(-1)
    weights = [
        coupling[l].reshape(peers, per_peer, boxes, rank, 2 * rank) for l in range(LEVELS)
    ]

    def six(x):
        return x.reshape(peers, per_peer, boxes, rank, x.shape[-1])

    first = six(coeffs[..., :LANES])
    second = six(coeffs[..., LANES : 2 * LANES])
    tail = six(coeffs[..., 2 * LANES :]).transpose(0, 2, 3, 1, 4).reshape(peers, boxes, rank, per_peer * tail_w)
    tail = jnp.pad(tail, ((0, 0), (0, 0), (0, 0), (0, LANES - per_peer * tail_w)))[:, None]

    low = range(half)
    high = range(half, per_peer)
    a0, a1 = run_level(
        0, tail_w, [[("m", 0, j, j) for j in low], [("m", 0, j, j) for j in high]],
        flat_pattern, weights[0], [first], [from_partner(first, 0)],
    )
    b0, b1 = run_level(
        0, tail_w,
        [[("t", 1, 0)] + [("m", 0, j, j) for j in low], [("m", 0, j, j) for j in high]],
        flat_pattern, weights[0], [second, tail], [from_partner(second, 0), from_partner(tail, 0)],
    )
    chunks = [a0, a1, b0, b1]
    slot_lists = [
        [("m", 0, j, j) for j in low],
        [("m", 0, j - half, j) for j in high],
        [("t", 0, 0)] + [("m", 0, 1 + j, j) for j in low],
        [("m", 0, j - half, j) for j in high],
    ]
    done = []
    for chunk, slots in zip(chunks, slot_lists):
        for lev in range(1, LEVELS):
            far = from_partner(chunk, lev)
            (chunk,) = run_level(lev, tail_w, [slots], flat_pattern, weights[lev], [chunk], [far])
        done.append(lax.all_to_all(chunk, "order", split_axis=0, concat_axis=0, tiled=True))
    me = lax.axis_index("order").astype(jnp.int32).reshape(1)
    return place(tail_w, me, assign, done, cols)


def solution(mesh):
    return jax.shard_map(
        per_device,
        mesh=mesh,
        in_specs=(
            P("order", "lat", None, None),
            P(None, "order", "lat", None, None),
            P(None, "order", "lat"),
            P(),
        ),
        out_specs=P("order", "lat", None, None),
        check_vma=False,
    )
```

```python
import functools

import jax
import jax.numpy as jnp
from jax import lax
from jax.experimental import pallas as pl
from jax.experimental.pallas import tpu as pltpu
from jax.sharding import PartitionSpec as P

LEVELS = 4
LANES = 128
TAIL = -1
PIECE = 8
FIRST = ((0, 1, 2), (3, 4, 5))
SECOND = ((-1, 0, 1, 2), (3, 4, 5))
ORDER = ((0, 1), (1, 1), (0, 2), (0, 3), (1, 2), (2, 1), (1, 3), (2, 2), (3, 1), (3, 2), (2, 3), (3, 3))
WAITS = {(2, 3): (0,), (3, 3): (0,)}
EARLY = (3, 3)


def from_partner(value, bit):
    size = lax.axis_size("lat")
    return lax.ppermute(value, "lat", [(i, i ^ 1 << bit) for i in range(size)])


def level_kernel(spec, lev, tail_w, pat_ref, w_ref, *refs):
    n_in = spec["n_in"]
    own, far, outs = refs[:n_in], refs[n_in : 2 * n_in], refs[-len(spec["slots"]) :]
    groups, per_peer = w_ref.shape[0], w_ref.shape[1]
    boxes = w_ref.shape[2]
    lane = lax.broadcasted_iota(jnp.int32, (w_ref.shape[3], LANES), 1)
    total = groups * per_peer

    def group(c, carry):
        for out, slots in zip(outs, spec["slots"]):
            for at, slot in enumerate(slots):
                for g in range(boxes):

                    def product(order, src, idx):
                        sel = pat_ref[(lev * total + c * per_peer + order) * boxes + g]
                        rhs = jnp.concatenate([own[src][c, idx, g], far[src][c, idx, sel]], axis=0)
                        return jnp.dot(w_ref[c, order, g], rhs, preferred_element_type=jnp.float32)

                    if slot[0] == "m":
                        acc = product(slot[3], slot[1], slot[2])
                    else:
                        acc = product(0, slot[1], slot[2])
                        for j in range(1, per_peer):
                            acc = jnp.where(lane < j * tail_w, acc, product(j, slot[1], slot[2]))
                    out[c, at, g] = acc.astype(jnp.bfloat16)
        return carry

    lax.fori_loop(0, groups, group, 0, unroll=4)


def run_level(lev, tail_w, slots, pattern, weights, own, far, after):
    peers, per_peer, boxes, rank, _ = weights.shape
    spec = {"n_in": len(own), "slots": slots}
    vmem = pl.BlockSpec(memory_space=pltpu.VMEM)
    out_shapes = [jax.ShapeDtypeStruct((peers, len(s), boxes, rank, LANES), jnp.bfloat16) for s in slots]
    return pl.pallas_call(
        functools.partial(level_kernel, spec, lev, tail_w),
        in_specs=[pl.BlockSpec(memory_space=pltpu.SMEM)]
        + [vmem] * (1 + 2 * len(own))
        + [pl.BlockSpec(memory_space=pl.ANY)] * len(after),
        out_specs=[vmem] * len(slots),
        out_shape=out_shapes,
        cost_estimate=pl.CostEstimate(flops=1, bytes_accessed=1, transcendentals=0),
    )(pattern, weights, *own, *far, *after)


def place_kernel(tail_w, slots, me_ref, assign_ref, *refs):
    out_ref = refs[-1]
    peers, per_peer, boxes = refs[0].shape[0], len(slots), refs[0].shape[2]
    local = peers * per_peer
    me = me_ref[0]

    def peer(k, carry):
        for j, (src, at) in enumerate(slots):
            to = assign_ref[k * local + me * per_peer + j] - me * local
            for g in range(boxes):
                value = refs[src][k, at, g]
                if out_ref.shape[-1] < LANES:
                    value = value.astype(jnp.float32)
                    if j:
                        value = pltpu.roll(value, LANES - j * tail_w, 1)
                    value = value[:, :tail_w].astype(jnp.bfloat16)
                out_ref[to, g] = value
        return carry

    lax.fori_loop(0, peers, peer, 0, unroll=2)


def place(tail_w, slots, me, assign, parts, cols, after=()):
    peers, _, boxes, rank, _ = parts[0].shape
    vmem = pl.BlockSpec(memory_space=pltpu.VMEM)
    smem = pl.BlockSpec(memory_space=pltpu.SMEM)
    return pl.pallas_call(
        functools.partial(place_kernel, tail_w, slots),
        in_specs=[smem, smem] + [vmem] * len(parts) + [pl.BlockSpec(memory_space=pl.ANY)] * len(after),
        out_specs=vmem,
        out_shape=jax.ShapeDtypeStruct((peers * len(slots), boxes, rank, cols), jnp.bfloat16),
        cost_estimate=pl.CostEstimate(flops=1, bytes_accessed=1, transcendentals=0),
    )(me, assign, *parts, *after)


def store_kernel(start, *refs):
    piece, out, sems = refs[0], refs[-2], refs[-1]
    boxes, width = piece.shape[:2]
    part = width // sems.shape[1]
    copies = [
        pltpu.make_async_copy(
            piece.at[g, pl.ds(q * part, part)], out.at[g, pl.ds(start + q * part, part)], sems.at[g, q]
        )
        for g in range(boxes)
        for q in range(sems.shape[1])
    ]
    for copy in copies:
        copy.start()
    for copy in copies:
        copy.wait()


def store(piece, start, cols, whole=None):
    boxes, _, rank, local = piece.shape
    held = [] if whole is None else [whole]
    return pl.pallas_call(
        functools.partial(store_kernel, start),
        in_specs=[pl.BlockSpec(memory_space=pltpu.VMEM)] + [pl.BlockSpec(memory_space=pl.ANY)] * len(held),
        out_specs=pl.BlockSpec(memory_space=pl.ANY),
        out_shape=jax.ShapeDtypeStruct((boxes, cols, rank, local), jnp.bfloat16),
        scratch_shapes=[pltpu.SemaphoreType.DMA((boxes, 4 if piece.shape[1] % 4 == 0 else 1))],
        input_output_aliases={1: 0} if held else {},
        cost_estimate=pl.CostEstimate(flops=1, bytes_accessed=1, transcendentals=0),
    )(piece, *held)


def per_device(coeffs, coupling, pattern, assign):
    local, boxes, rank, cols = coeffs.shape
    peers = lax.axis_size("order")
    per_peer = local // peers
    tail_w = cols - 2 * LANES
    me = lax.axis_index("order").astype(jnp.int32).reshape(1)

    def six(x):
        return x.reshape(peers, per_peer, boxes, rank, x.shape[-1])

    def level_weights(c, l):
        return six(c[l])

    first = six(coeffs[..., :LANES])
    coeffs, coupling_later, first = lax.optimization_barrier((coeffs, coupling, first))
    first_far = from_partner(first, 0)
    weights = [level_weights(coupling, 0)] + [level_weights(coupling_later, l) for l in range(1, LEVELS)]
    flat_pattern = pattern.reshape(-1)

    after = []

    def level(lev, slots, own, far):
        outs = run_level(lev, tail_w, slots, flat_pattern, weights[lev], own, far, after)
        after[:] = outs[:1]
        return outs

    def split(groups, tail_at):
        return [[("t", tail_at, 0) if j == TAIL else ("m", 0, j, j) for j in group] for group in groups]

    def own_slots(group):
        return [("t", 0, i) if j == TAIL else ("m", 0, i, j) for i, j in enumerate(group)]

    def places(groups):
        found = {j: (at, i) for at, group in enumerate(groups) for i, j in enumerate(group)}
        return [found[j] for j in range(per_peer)]

    chunks = list(level(0, split(FIRST, 0), [first], [first_far]))
    second = six(coeffs[..., LANES : 2 * LANES])
    tail = six(coeffs[..., 2 * LANES :]).transpose(0, 2, 3, 1, 4).reshape(peers, boxes, rank, per_peer * tail_w)
    tail = jnp.pad(tail, ((0, 0), (0, 0), (0, 0), (0, LANES - per_peer * tail_w)))[:, None]
    chunks += level(
        0, split(SECOND, 1), [second, tail], [from_partner(second, 0), from_partner(tail, 0)]
    )
    groups = FIRST + SECOND
    tail_chunk = [TAIL in group for group in groups].index(True)
    far = [[from_partner(chunk, 1)] for chunk in chunks]
    chunks = [[chunk] for chunk in chunks]
    where = [own_slots(group) for group in groups]
    done = [None] * len(chunks)
    whole = None
    for k, lev in ORDER:
        if (k, lev) == EARLY:
            early = place(tail_w, places(FIRST), me, assign, done[: len(FIRST)], LANES)
            whole = store(early.transpose(1, 3, 2, 0), 0, cols)
            after.append(whole)
        after += [done[w] for w in WAITS.get((k, lev), ())]
        width = PIECE if lev + 1 < LEVELS else len(where[k])
        pieces = [where[k][i : i + width] for i in range(0, len(where[k]), width)]
        chunks[k] = level(lev, pieces, chunks[k], far[k])
        if lev + 1 < LEVELS:
            far[k] = [from_partner(piece, lev + 1) for piece in chunks[k]]
            where[k] = [
                slot[:1] + (at, i) + slot[3:] for at, piece in enumerate(pieces) for i, slot in enumerate(piece)
            ]
        else:
            done[k] = lax.all_to_all(chunks[k][0], "order", split_axis=0, concat_axis=0, tiled=True)
    tail_slot = groups[tail_chunk].index(TAIL)
    ends = place(tail_w, [(0, tail_slot)] * per_peer, me, assign, [done[tail_chunk]], tail_w, after)
    whole = store(ends.transpose(1, 3, 2, 0), 2 * LANES, cols, whole)
    late = place(tail_w, places(SECOND), me, assign, done[len(FIRST) :], LANES, [whole])
    whole = store(late.transpose(1, 3, 2, 0), LANES, cols, whole)
    return whole.transpose(3, 0, 2, 1)


def solution(mesh):
    return jax.shard_map(
        per_device,
        mesh=mesh,
        in_specs=(
            P("order", "lat", None, None),
            P(None, "order", "lat", None, None),
            P(None, "order", "lat"),
            P(),
        ),
        out_specs=P("order", "lat", None, None),
        check_vma=False,
    )
```

```python
import functools

import jax
import jax.numpy as jnp
from jax import lax
from jax.experimental import pallas as pl
from jax.experimental.pallas import tpu as pltpu
from jax.sharding import PartitionSpec as P

LANES = 128
TAIL = -1
FIRST = ((0, 1, 2, 3, 4, 5),)
SECOND = ((-1, 0, 1, 2), (3, 4, 5))
ORDER = ((0, 1), (0, 2), (1, 1), (1, 2), (2, 1), (0, 3), (2, 2), (1, 3), (2, 3))
WAITS = {}
EARLY = (2, 3)


def from_partner(value, mask):
    size = lax.axis_size("lat")
    return lax.ppermute(value, "lat", [(i, i ^ mask) for i in range(size)])


def product(weights, own, far):
    rhs = jnp.concatenate([own, far], axis=0)
    return jnp.dot(weights, rhs, preferred_element_type=jnp.float32)


def slot_value(slot, tail_w, per_peer, rank, term):
    if slot[0] == "m":
        return term(slot[3]).astype(jnp.bfloat16)
    lane = lax.broadcasted_iota(jnp.int32, (rank, LANES), 1)
    acc = term(0)
    for order in range(1, per_peer):
        acc = jnp.where(lane < order * tail_w, acc, term(order))
    return acc.astype(jnp.bfloat16)


def level_kernel(spec, lev, tail_w, at_ref, pat_ref, w_ref, *refs):
    n_in = spec["n_in"]
    own, far, outs = refs[:n_in], refs[n_in : 2 * n_in], refs[-spec["n_out"] :]
    peers, per_peer, boxes, rank = w_ref.shape[:4]
    total = peers * per_peer

    def group(out, slots, c, row):
        for at, slot in enumerate(slots):
            for g in range(boxes):

                def term(order):
                    sel = pat_ref[(lev * total + c * per_peer + order) * boxes + g]
                    mine, other = own[slot[1]], far[slot[1]]
                    return product(w_ref[c, order, g], mine[c, slot[2], g], other[c, slot[2], sel])

                out[row, at, g] = slot_value(slot, tail_w, per_peer, rank, term)

    if spec["spread"]:
        part = peers // len(outs)
        for d, out in enumerate(outs):
            first = (at_ref[1] ^ d) * part

            def body(i, carry):
                group(out, spec["slots"][0], first + i, i)
                return carry

            lax.fori_loop(0, part, body, 0, unroll=2)
    else:

        def body(c, carry):
            for out, slots in zip(outs, spec["slots"]):
                group(out, slots, c, c)
            return carry

        lax.fori_loop(0, peers, body, 0, unroll=4)


SMEM = pl.BlockSpec(memory_space=pltpu.SMEM)
VMEM = pl.BlockSpec(memory_space=pltpu.VMEM)
ANY = pl.BlockSpec(memory_space=pl.ANY)
CHEAP = pl.CostEstimate(flops=1, bytes_accessed=1, transcendentals=0)


def run_level(lev, tail_w, slots, at, pattern, weights, own, far, after, spread):
    peers, _, boxes, rank, _ = weights.shape
    shapes = [(peers, len(s), boxes, rank, LANES) for s in slots]
    if spread:
        shapes = [(peers // spread, *shapes[0][1:])] * spread
    spec = {"n_in": len(own), "slots": slots, "spread": spread, "n_out": len(shapes)}
    return pl.pallas_call(
        functools.partial(level_kernel, spec, lev, tail_w),
        in_specs=[SMEM, SMEM] + [VMEM] * (1 + 2 * len(own)) + [ANY] * len(after),
        out_specs=[VMEM] * len(shapes),
        out_shape=[jax.ShapeDtypeStruct(shape, jnp.bfloat16) for shape in shapes],
        cost_estimate=CHEAP,
    )(at, pattern, weights, *own, *far, *after)


def pack_kernel(at_ref, low_ref, high_ref, *outs):
    part = outs[0].shape[0]
    half = low_ref.shape[-1]
    for d, out in enumerate(outs):
        first = (at_ref[1] ^ d) * part
        out[:, :, :, :, :half] = low_ref[pl.ds(first, part)]
        out[:, :, :, :, half:] = high_ref[pl.ds(first, part)]


def pack(at, low, high, ys):
    peers, per_peer, boxes, rank, half = low.shape
    shape = jax.ShapeDtypeStruct((peers // ys, per_peer, boxes, rank, 2 * half), jnp.bfloat16)
    return pl.pallas_call(
        pack_kernel,
        in_specs=[SMEM, VMEM, VMEM],
        out_specs=[VMEM] * ys,
        out_shape=[shape] * ys,
        cost_estimate=CHEAP,
    )(at, low, high)


def last_kernel(spec, tail_w, pat_ref, *refs):
    ys, slots = spec["ys"], spec["slots"]
    weights, blocks = refs[:ys], refs[ys : 2 * ys]
    outs, mid = refs[-ys - 1 : -1], refs[-1]
    part, per_peer, boxes, rank, width = weights[0].shape
    half = width // 2

    def level(step, i, source, target):
        for d in range(ys):
            for at, slot in enumerate(slots):
                for g in range(boxes):

                    def term(order):
                        sel = pat_ref[(((d * 2 + step) * part + i) * per_peer + order) * boxes + g]
                        w = weights[d][i, order, g][:, step * half : (step + 1) * half]
                        return product(w, source(d)[i, at, g], source(d ^ (1 + step))[i, at, sel])

                    target(d)[i, at, g] = slot_value(slot, tail_w, per_peer, rank, term)

    def first(i, carry):
        level(0, i, lambda d: blocks[d], lambda d: mid.at[d])
        return carry

    def second(i, carry):
        level(1, i, lambda d: mid.at[d], lambda d: outs[d])
        return carry

    lax.fori_loop(0, part, first, 0)
    lax.fori_loop(0, part, second, 0)


def run_last(tail_w, slots, pattern, weights, blocks, after):
    ys = len(blocks)
    shape = jax.ShapeDtypeStruct(blocks[0].shape, jnp.bfloat16)
    return pl.pallas_call(
        functools.partial(last_kernel, {"ys": ys, "slots": slots}, tail_w),
        in_specs=[SMEM] + [VMEM] * (2 * ys) + [ANY] * len(after),
        out_specs=[VMEM] * ys,
        out_shape=[shape] * ys,
        scratch_shapes=[pltpu.VMEM((ys, *blocks[0].shape), jnp.bfloat16)],
        cost_estimate=CHEAP,
    )(pattern, *weights, *blocks, *after)


def join_kernel(ys, at_ref, *refs):
    out = refs[-1]
    part = refs[0].shape[0]
    for d in range(ys):
        first = (at_ref[1] ^ d) * part
        out[pl.ds(first, part)] = refs[d][...]


def join(at, parts, after):
    ys = len(parts)
    part, *rest = parts[0].shape
    return pl.pallas_call(
        functools.partial(join_kernel, ys),
        in_specs=[SMEM] + [VMEM] * ys + [ANY] * len(after),
        out_specs=VMEM,
        out_shape=jax.ShapeDtypeStruct((ys * part, *rest), jnp.bfloat16),
        cost_estimate=CHEAP,
    )(at, *parts, *after)


def place_kernel(tail_w, slots, me_ref, assign_ref, *refs):
    out_ref = refs[-1]
    peers, per_peer, boxes = refs[0].shape[0], len(slots), refs[0].shape[2]
    local = peers * per_peer
    me = me_ref[0]

    def peer(k, carry):
        for j, (src, at) in enumerate(slots):
            to = assign_ref[k * local + me * per_peer + j] - me * local
            for g in range(boxes):
                value = refs[src][k, at, g]
                if out_ref.shape[-1] < LANES:
                    value = value.astype(jnp.float32)
                    if j:
                        value = pltpu.roll(value, LANES - j * tail_w, 1)
                    value = value[:, :tail_w].astype(jnp.bfloat16)
                out_ref[to, g] = value
        return carry

    lax.fori_loop(0, peers, peer, 0, unroll=2)


def place(tail_w, slots, parts, me, assign, cols, after=()):
    peers, _, boxes, rank, _ = parts[0].shape
    vmem = pl.BlockSpec(memory_space=pltpu.VMEM)
    smem = pl.BlockSpec(memory_space=pltpu.SMEM)
    return pl.pallas_call(
        functools.partial(place_kernel, tail_w, slots),
        in_specs=[smem, smem] + [vmem] * len(parts) + [pl.BlockSpec(memory_space=pl.ANY)] * len(after),
        out_specs=vmem,
        out_shape=jax.ShapeDtypeStruct((peers * len(slots), boxes, rank, cols), jnp.bfloat16),
        cost_estimate=pl.CostEstimate(flops=1, bytes_accessed=1, transcendentals=0),
    )(me, assign, *parts, *after)


def store_kernel(start, *refs):
    piece, out, sems = refs[0], refs[-2], refs[-1]
    boxes, width = piece.shape[:2]
    part = width // sems.shape[1]
    copies = [
        pltpu.make_async_copy(
            piece.at[g, pl.ds(q * part, part)], out.at[g, pl.ds(start + q * part, part)], sems.at[g, q]
        )
        for g in range(boxes)
        for q in range(sems.shape[1])
    ]
    for copy in copies:
        copy.start()
    for copy in copies:
        copy.wait()


def store(piece, start, cols, whole=None):
    boxes, _, rank, local = piece.shape
    held = [] if whole is None else [whole]
    return pl.pallas_call(
        functools.partial(store_kernel, start),
        in_specs=[pl.BlockSpec(memory_space=pltpu.VMEM)] + [pl.BlockSpec(memory_space=pl.ANY)] * len(held),
        out_specs=pl.BlockSpec(memory_space=pl.ANY),
        out_shape=jax.ShapeDtypeStruct((boxes, cols, rank, local), jnp.bfloat16),
        scratch_shapes=[pltpu.SemaphoreType.DMA((boxes, 4 if piece.shape[1] % 4 == 0 else 1))],
        input_output_aliases={1: 0} if held else {},
        cost_estimate=pl.CostEstimate(flops=1, bytes_accessed=1, transcendentals=0),
    )(piece, *held)


def per_device(coeffs, coupling, pattern, assign):
    local, boxes, rank, cols = coeffs.shape
    peers = lax.axis_size("order")
    per_peer = local // peers
    tail_w = cols - 2 * LANES
    order_at = lax.axis_index("order").astype(jnp.int32)
    lat_at = lax.axis_index("lat").astype(jnp.int32)
    ys = lax.axis_size("lat") >> 2
    me = jnp.stack([order_at, lat_at >> 2])

    def six(x):
        return x.reshape(peers, per_peer, boxes, rank, x.shape[-1])

    def level_weights(c, l):
        return six(c[l])

    first = six(coeffs[..., :LANES])
    coeffs, coupling_later, first = lax.optimization_barrier((coeffs, coupling, first))
    first_far = from_partner(first, 1)
    weights = [level_weights(coupling, 0)] + [level_weights(coupling_later, l) for l in range(1, coupling.shape[0])]
    flat_pattern = pattern.reshape(-1)

    after = []

    def level(lev, slots, own, far, spread=0):
        outs = run_level(lev, tail_w, slots, me, flat_pattern, weights[lev], own, far, after, spread)
        after[:] = outs[:1]
        return outs

    def split(groups, tail_at):
        return [[("t", tail_at, 0) if j == TAIL else ("m", 0, j, j) for j in group] for group in groups]

    def own_slots(group):
        return [("t", 0, i) if j == TAIL else ("m", 0, i, j) for i, j in enumerate(group)]

    def places(members):
        arrays, found = [], {}
        for m in members:
            array, offset = done[m]
            if not arrays or arrays[-1] is not array:
                arrays.append(array)
            for i, j in enumerate(groups[m]):
                found[j] = (len(arrays) - 1, offset + i)
        return [found[j] for j in range(per_peer)], arrays

    chunks = list(level(0, split(FIRST, 0), [first], [first_far]))
    second = six(coeffs[..., LANES : 2 * LANES])
    tail = six(coeffs[..., 2 * LANES :]).transpose(0, 2, 3, 1, 4).reshape(peers, boxes, rank, per_peer * tail_w)
    tail = jnp.pad(tail, ((0, 0), (0, 0), (0, 0), (0, LANES - per_peer * tail_w)))[:, None]
    chunks += level(
        0, split(SECOND, 1), [second, tail], [from_partner(second, 1), from_partner(tail, 1)]
    )
    groups = FIRST + SECOND
    tail_chunk = [TAIL in group for group in groups].index(True)
    far = [from_partner(chunk, 2) for chunk in chunks]
    packed = pack(me, weights[2], weights[3], ys)
    packed = [packed[0]] + [from_partner(packed[d], 4 * d) for d in range(1, ys)]
    after.append(packed[0])
    by_peer = pattern[2:].reshape(2, ys, -1).transpose(1, 0, 2).reshape(ys, -1)
    choices = [lax.dynamic_index_in_dim(by_peer, me[1] ^ d, 0, keepdims=False) for d in range(ys)]
    choices = jnp.concatenate([choices[0]] + [from_partner(choices[d], 4 * d) for d in range(1, ys)])

    where = [own_slots(group) for group in groups]
    done = [None] * len(chunks)
    whole = None
    for k, step in ORDER:
        if (k, step) == EARLY:
            early = place(tail_w, *places(range(len(FIRST))), me, assign, LANES)
            whole = store(early.transpose(1, 3, 2, 0), 0, cols)
            after.append(whole)
        after += [done[w][0] for w in WAITS.get((k, step), ())]
        if step == 1:
            outs = level(1, [where[k]], [chunks[k]], [far[k]], ys)
        elif step == 2:
            outs = run_last(tail_w, where[k], choices, packed, chunks[k], after)
        else:
            outs = [join(me, chunks[k], after)]
            done[k] = (lax.all_to_all(outs[0], "order", split_axis=0, concat_axis=0, tiled=True), 0)
        after[:] = outs[:1]
        chunks[k] = [outs[0]] + [from_partner(out, 4 * (d + 1)) for d, out in enumerate(outs[1:])]
    array, offset = done[tail_chunk]
    tail_slot = offset + groups[tail_chunk].index(TAIL)
    ends = place(tail_w, [(0, tail_slot)] * per_peer, [array], me, assign, tail_w, after)
    whole = store(ends.transpose(1, 3, 2, 0), 2 * LANES, cols, whole)
    late = place(tail_w, *places(range(len(FIRST), len(groups))), me, assign, LANES, [whole])
    whole = store(late.transpose(1, 3, 2, 0), LANES, cols, whole)
    return whole.transpose(3, 0, 2, 1)


def solution(mesh):
    return jax.shard_map(
        per_device,
        mesh=mesh,
        in_specs=(
            P("order", "lat", None, None),
            P(None, "order", "lat", None, None),
            P(None, "order", "lat"),
            P(),
        ),
        out_specs=P("order", "lat", None, None),
        check_vma=False,
    )
```

```python
import functools

import jax
import jax.numpy as jnp
from jax import lax
from jax.experimental import pallas as pl
from jax.experimental.pallas import tpu as pltpu
from jax.sharding import PartitionSpec as P

LANES = 128
TAIL = -1
FIRST = ((0, 1, 2, 3, 4, 5),)
SECOND = ((-1, 0, 1, 2), (3, 4, 5))
ORDER = ((0, 1), (0, 2), (1, 1), (2, 1), (0, 3), (1, 2), (2, 2), (1, 3), (2, 3))
WAITS = {}
BEHIND = {(0, 3): (1,), (1, 2): (2,)}
EARLY = (2, 3)


def from_partner(value, mask):
    size = lax.axis_size("lat")
    return lax.ppermute(value, "lat", [(i, i ^ mask) for i in range(size)])


def product(weights, own, far):
    rhs = jnp.concatenate([own, far], axis=0)
    return jnp.dot(weights, rhs, preferred_element_type=jnp.float32)


def slot_value(slot, tail_w, per_peer, rank, term):
    if slot[0] == "m":
        return term(slot[3]).astype(jnp.bfloat16)
    lane = lax.broadcasted_iota(jnp.int32, (rank, LANES), 1)
    acc = term(0)
    for order in range(1, per_peer):
        acc = jnp.where(lane < order * tail_w, acc, term(order))
    return acc.astype(jnp.bfloat16)


def level_kernel(spec, lev, tail_w, at_ref, pat_ref, w_ref, *refs):
    n_in = spec["n_in"]
    own, far, outs = refs[:n_in], refs[n_in : 2 * n_in], refs[-spec["n_out"] :]
    peers, per_peer, boxes, rank = w_ref.shape[:4]
    total = peers * per_peer

    def group(out, slots, c, row):
        for at, slot in enumerate(slots):
            for g in range(boxes):

                def term(order):
                    sel = pat_ref[(lev * total + c * per_peer + order) * boxes + g]
                    mine, other = own[slot[1]], far[slot[1]]
                    return product(w_ref[c, order, g], mine[c, slot[2], g], other[c, slot[2], sel])

                out[row, at, g] = slot_value(slot, tail_w, per_peer, rank, term)

    if spec["spread"]:
        part = peers // len(outs)
        for d, out in enumerate(outs):
            first = (at_ref[1] ^ d) * part

            def body(i, carry):
                group(out, spec["slots"][0], first + i, i)
                return carry

            lax.fori_loop(0, part, body, 0, unroll=2)
    else:

        def body(c, carry):
            for out, slots in zip(outs, spec["slots"]):
                group(out, slots, c, c)
            return carry

        lax.fori_loop(0, peers, body, 0, unroll=4)


SMEM = pl.BlockSpec(memory_space=pltpu.SMEM)
VMEM = pl.BlockSpec(memory_space=pltpu.VMEM)
ANY = pl.BlockSpec(memory_space=pl.ANY)
CHEAP = pl.CostEstimate(flops=1, bytes_accessed=1, transcendentals=0)


def run_level(lev, tail_w, slots, at, pattern, weights, own, far, after, spread):
    peers, _, boxes, rank, _ = weights.shape
    shapes = [(peers, len(s), boxes, rank, LANES) for s in slots]
    if spread:
        shapes = [(peers // spread, *shapes[0][1:])] * spread
    spec = {"n_in": len(own), "slots": slots, "spread": spread, "n_out": len(shapes)}
    return pl.pallas_call(
        functools.partial(level_kernel, spec, lev, tail_w),
        in_specs=[SMEM, SMEM] + [VMEM] * (1 + 2 * len(own)) + [ANY] * len(after),
        out_specs=[VMEM] * len(shapes),
        out_shape=[jax.ShapeDtypeStruct(shape, jnp.bfloat16) for shape in shapes],
        cost_estimate=CHEAP,
    )(at, pattern, weights, *own, *far, *after)


def pack_kernel(at_ref, low_ref, high_ref, *outs):
    part = outs[0].shape[0]
    half = low_ref.shape[-1]
    for d, out in enumerate(outs):
        first = (at_ref[1] ^ d) * part
        out[:, :, :, :, :half] = low_ref[pl.ds(first, part)]
        out[:, :, :, :, half:] = high_ref[pl.ds(first, part)]


def pack(at, low, high, ys):
    peers, per_peer, boxes, rank, half = low.shape
    shape = jax.ShapeDtypeStruct((peers // ys, per_peer, boxes, rank, 2 * half), jnp.bfloat16)
    return pl.pallas_call(
        pack_kernel,
        in_specs=[SMEM, VMEM, VMEM],
        out_specs=[VMEM] * ys,
        out_shape=[shape] * ys,
        cost_estimate=CHEAP,
    )(at, low, high)


def last_kernel(spec, tail_w, pat_ref, *refs):
    ys, slots = spec["ys"], spec["slots"]
    weights, blocks = refs[:ys], refs[ys : 2 * ys]
    outs, mid = refs[-ys - 1 : -1], refs[-1]
    part, per_peer, boxes, rank, width = weights[0].shape
    half = width // 2

    def level(step, i, source, target):
        for d in range(ys):
            for at, slot in enumerate(slots):
                for g in range(boxes):

                    def term(order):
                        sel = pat_ref[(((d * 2 + step) * part + i) * per_peer + order) * boxes + g]
                        w = weights[d][i, order, g][:, step * half : (step + 1) * half]
                        return product(w, source(d)[i, at, g], source(d ^ (1 + step))[i, at, sel])

                    target(d)[i, at, g] = slot_value(slot, tail_w, per_peer, rank, term)

    def first(i, carry):
        level(0, i, lambda d: blocks[d], lambda d: mid.at[d])
        return carry

    def second(i, carry):
        level(1, i, lambda d: mid.at[d], lambda d: outs[d])
        return carry

    lax.fori_loop(0, part, first, 0)
    lax.fori_loop(0, part, second, 0)


def run_last(tail_w, slots, pattern, weights, blocks, after):
    ys = len(blocks)
    shape = jax.ShapeDtypeStruct(blocks[0].shape, jnp.bfloat16)
    return pl.pallas_call(
        functools.partial(last_kernel, {"ys": ys, "slots": slots}, tail_w),
        in_specs=[SMEM] + [VMEM] * (2 * ys) + [ANY] * len(after),
        out_specs=[VMEM] * ys,
        out_shape=[shape] * ys,
        scratch_shapes=[pltpu.VMEM((ys, *blocks[0].shape), jnp.bfloat16)],
        cost_estimate=CHEAP,
    )(pattern, *weights, *blocks, *after)


def join_kernel(ys, at_ref, *refs):
    out = refs[-1]
    part = refs[0].shape[0]
    for d in range(ys):
        first = (at_ref[1] ^ d) * part
        out[pl.ds(first, part)] = refs[d][...]


def join(at, parts, after):
    ys = len(parts)
    part, *rest = parts[0].shape
    return pl.pallas_call(
        functools.partial(join_kernel, ys),
        in_specs=[SMEM] + [VMEM] * ys + [ANY] * len(after),
        out_specs=VMEM,
        out_shape=jax.ShapeDtypeStruct((ys * part, *rest), jnp.bfloat16),
        cost_estimate=CHEAP,
    )(at, *parts, *after)


def place_kernel(tail_w, slots, me_ref, assign_ref, *refs):
    out_ref = refs[-1]
    peers, per_peer, boxes = refs[0].shape[0], len(slots), refs[0].shape[2]
    local = peers * per_peer
    me = me_ref[0]

    def peer(k, carry):
        for j, (src, at) in enumerate(slots):
            to = assign_ref[k * local + me * per_peer + j] - me * local
            for g in range(boxes):
                value = refs[src][k, at, g]
                if out_ref.shape[-1] < LANES:
                    value = value.astype(jnp.float32)
                    if j:
                        value = pltpu.roll(value, LANES - j * tail_w, 1)
                    value = value[:, :tail_w].astype(jnp.bfloat16)
                out_ref[to, g] = value
        return carry

    lax.fori_loop(0, peers, peer, 0, unroll=2)


def place(tail_w, slots, parts, me, assign, cols, after=()):
    peers, _, boxes, rank, _ = parts[0].shape
    vmem = pl.BlockSpec(memory_space=pltpu.VMEM)
    smem = pl.BlockSpec(memory_space=pltpu.SMEM)
    return pl.pallas_call(
        functools.partial(place_kernel, tail_w, slots),
        in_specs=[smem, smem] + [vmem] * len(parts) + [pl.BlockSpec(memory_space=pl.ANY)] * len(after),
        out_specs=vmem,
        out_shape=jax.ShapeDtypeStruct((peers * len(slots), boxes, rank, cols), jnp.bfloat16),
        cost_estimate=pl.CostEstimate(flops=1, bytes_accessed=1, transcendentals=0),
    )(me, assign, *parts, *after)


def store_kernel(start, *refs):
    piece, out, sems = refs[0], refs[-2], refs[-1]
    boxes, width = piece.shape[:2]
    part = width // sems.shape[1]
    copies = [
        pltpu.make_async_copy(
            piece.at[g, pl.ds(q * part, part)], out.at[g, pl.ds(start + q * part, part)], sems.at[g, q]
        )
        for g in range(boxes)
        for q in range(sems.shape[1])
    ]
    for copy in copies:
        copy.start()
    for copy in copies:
        copy.wait()


def store(piece, start, cols, whole=None):
    boxes, _, rank, local = piece.shape
    held = [] if whole is None else [whole]
    return pl.pallas_call(
        functools.partial(store_kernel, start),
        in_specs=[pl.BlockSpec(memory_space=pltpu.VMEM)] + [pl.BlockSpec(memory_space=pl.ANY)] * len(held),
        out_specs=pl.BlockSpec(memory_space=pl.ANY),
        out_shape=jax.ShapeDtypeStruct((boxes, cols, rank, local), jnp.bfloat16),
        scratch_shapes=[pltpu.SemaphoreType.DMA((boxes, 4 if piece.shape[1] % 4 == 0 else 1))],
        input_output_aliases={1: 0} if held else {},
        cost_estimate=pl.CostEstimate(flops=1, bytes_accessed=1, transcendentals=0),
    )(piece, *held)


def per_device(coeffs, coupling, pattern, assign):
    local, boxes, rank, cols = coeffs.shape
    peers = lax.axis_size("order")
    per_peer = local // peers
    tail_w = cols - 2 * LANES
    order_at = lax.axis_index("order").astype(jnp.int32)
    lat_at = lax.axis_index("lat").astype(jnp.int32)
    ys = lax.axis_size("lat") >> 2
    me = jnp.stack([order_at, lat_at >> 2])

    def six(x):
        return x.reshape(peers, per_peer, boxes, rank, x.shape[-1])

    def level_weights(c, l):
        return six(c[l])

    first = six(coeffs[..., :LANES])
    coeffs, coupling_later, first = lax.optimization_barrier((coeffs, coupling, first))
    first_far = from_partner(first, 1)
    weights = [level_weights(coupling, 0)] + [level_weights(coupling_later, l) for l in range(1, coupling.shape[0])]
    flat_pattern = pattern.reshape(-1)

    after = []

    def level(lev, slots, own, far, spread=0):
        outs = run_level(lev, tail_w, slots, me, flat_pattern, weights[lev], own, far, after, spread)
        after[:] = outs[:1]
        return outs

    def split(groups, tail_at):
        return [[("t", tail_at, 0) if j == TAIL else ("m", 0, j, j) for j in group] for group in groups]

    def own_slots(group):
        return [("t", 0, i) if j == TAIL else ("m", 0, i, j) for i, j in enumerate(group)]

    def places(members):
        arrays, found = [], {}
        for m in members:
            array, offset = done[m]
            if not arrays or arrays[-1] is not array:
                arrays.append(array)
            for i, j in enumerate(groups[m]):
                found[j] = (len(arrays) - 1, offset + i)
        return [found[j] for j in range(per_peer)], arrays

    chunks = list(level(0, split(FIRST, 0), [first], [first_far]))
    second = six(coeffs[..., LANES : 2 * LANES])
    tail = six(coeffs[..., 2 * LANES :]).transpose(0, 2, 3, 1, 4).reshape(peers, boxes, rank, per_peer * tail_w)
    tail = jnp.pad(tail, ((0, 0), (0, 0), (0, 0), (0, LANES - per_peer * tail_w)))[:, None]
    chunks += level(
        0, split(SECOND, 1), [second, tail], [from_partner(second, 1), from_partner(tail, 1)]
    )
    groups = FIRST + SECOND
    tail_chunk = [TAIL in group for group in groups].index(True)
    far = [from_partner(chunk, 2) for chunk in chunks]
    packed = pack(me, weights[2], weights[3], ys)
    packed = [packed[0]] + [from_partner(packed[d], 4 * d) for d in range(1, ys)]
    after.append(packed[0])
    by_peer = pattern[2:].reshape(2, ys, -1).transpose(1, 0, 2).reshape(ys, -1)
    choices = [lax.dynamic_index_in_dim(by_peer, me[1] ^ d, 0, keepdims=False) for d in range(ys)]
    choices = jnp.concatenate([choices[0]] + [from_partner(choices[d], 4 * d) for d in range(1, ys)])

    where = [own_slots(group) for group in groups]
    done = [None] * len(chunks)
    whole = None
    for k, step in ORDER:
        if (k, step) == EARLY:
            early = place(tail_w, *places(range(len(FIRST))), me, assign, LANES)
            whole = store(early.transpose(1, 3, 2, 0), 0, cols)
            after.append(whole)
        after += [done[w][0] for w in WAITS.get((k, step), ())]
        after += [piece for w in BEHIND.get((k, step), ()) for piece in chunks[w][1:]]
        if step == 1:
            outs = level(1, [where[k]], [chunks[k]], [far[k]], ys)
        elif step == 2:
            outs = run_last(tail_w, where[k], choices, packed, chunks[k], after)
        else:
            outs = [join(me, chunks[k], after)]
            done[k] = (lax.all_to_all(outs[0], "order", split_axis=0, concat_axis=0, tiled=True), 0)
        after[:] = outs[:1]
        chunks[k] = [outs[0]] + [from_partner(out, 4 * (d + 1)) for d, out in enumerate(outs[1:])]
    array, offset = done[tail_chunk]
    tail_slot = offset + groups[tail_chunk].index(TAIL)
    ends = place(tail_w, [(0, tail_slot)] * per_peer, [array], me, assign, tail_w, after)
    whole = store(ends.transpose(1, 3, 2, 0), 2 * LANES, cols, whole)
    late = place(tail_w, *places(range(len(FIRST), len(groups))), me, assign, LANES, [whole])
    whole = store(late.transpose(1, 3, 2, 0), LANES, cols, whole)
    return whole.transpose(3, 0, 2, 1)


def solution(mesh):
    return jax.shard_map(
        per_device,
        mesh=mesh,
        in_specs=(
            P("order", "lat", None, None),
            P(None, "order", "lat", None, None),
            P(None, "order", "lat"),
            P(),
        ),
        out_specs=P("order", "lat", None, None),
        check_vma=False,
    )
```

```python
import functools

import jax
import jax.numpy as jnp
from jax import lax
from jax.experimental import pallas as pl
from jax.experimental.pallas import tpu as pltpu
from jax.sharding import PartitionSpec as P

LANES = 128
TAIL = -1
FIRST = ((0, 1, 2, 3, 4, 5),)
SECOND = ((-1, 0, 1, 2), (3, 4, 5))
ORDER = ((0, 1), (0, 2), (1, 1), (0, 3), (2, 1), (1, 2), (2, 2), (1, 3), (2, 3))
WAITS = {}
BEHIND = {(0, 3): (2,)}
EARLY = (2, 3)


def from_partner(value, mask):
    size = lax.axis_size("lat")
    return lax.ppermute(value, "lat", [(i, i ^ mask) for i in range(size)])


def product(weights, own, far):
    rhs = jnp.concatenate([own, far], axis=0)
    return jnp.dot(weights, rhs, preferred_element_type=jnp.float32)


def slot_value(slot, tail_w, per_peer, rank, term):
    if slot[0] == "m":
        return term(slot[3]).astype(jnp.bfloat16)
    lane = lax.broadcasted_iota(jnp.int32, (rank, LANES), 1)
    acc = term(0)
    for order in range(1, per_peer):
        acc = jnp.where(lane < order * tail_w, acc, term(order))
    return acc.astype(jnp.bfloat16)


def level_kernel(spec, lev, tail_w, at_ref, pat_ref, w_ref, *refs):
    n_in = spec["n_in"]
    own, far, outs = refs[:n_in], refs[n_in : 2 * n_in], refs[-spec["n_out"] :]
    peers, per_peer, boxes, rank = w_ref.shape[:4]
    total = peers * per_peer

    def group(out, slots, c, row):
        for at, slot in enumerate(slots):
            for g in range(boxes):

                def term(order):
                    sel = pat_ref[(lev * total + c * per_peer + order) * boxes + g]
                    mine, other = own[slot[1]], far[slot[1]]
                    return product(w_ref[c, order, g], mine[c, slot[2], g], other[c, slot[2], sel])

                out[row, at, g] = slot_value(slot, tail_w, per_peer, rank, term)

    if spec["spread"]:
        part = peers // len(outs)
        for d, out in enumerate(outs):
            first = (at_ref[1] ^ d) * part

            def body(i, carry):
                group(out, spec["slots"][0], first + i, i)
                return carry

            lax.fori_loop(0, part, body, 0, unroll=2)
    else:

        def body(c, carry):
            for out, slots in zip(outs, spec["slots"]):
                group(out, slots, c, c)
            return carry

        lax.fori_loop(0, peers, body, 0, unroll=4)


SMEM = pl.BlockSpec(memory_space=pltpu.SMEM)
VMEM = pl.BlockSpec(memory_space=pltpu.VMEM)
ANY = pl.BlockSpec(memory_space=pl.ANY)
CHEAP = pl.CostEstimate(flops=1, bytes_accessed=1, transcendentals=0)


def run_level(lev, tail_w, slots, at, pattern, weights, own, far, after, spread):
    peers, _, boxes, rank, _ = weights.shape
    shapes = [(peers, len(s), boxes, rank, LANES) for s in slots]
    if spread:
        shapes = [(peers // spread, *shapes[0][1:])] * spread
    spec = {"n_in": len(own), "slots": slots, "spread": spread, "n_out": len(shapes)}
    return pl.pallas_call(
        functools.partial(level_kernel, spec, lev, tail_w),
        in_specs=[SMEM, SMEM] + [VMEM] * (1 + 2 * len(own)) + [ANY] * len(after),
        out_specs=[VMEM] * len(shapes),
        out_shape=[jax.ShapeDtypeStruct(shape, jnp.bfloat16) for shape in shapes],
        cost_estimate=CHEAP,
    )(at, pattern, weights, *own, *far, *after)


def pack_kernel(at_ref, low_ref, high_ref, *outs):
    part = outs[0].shape[0]
    half = low_ref.shape[-1]
    for d, out in enumerate(outs):
        first = (at_ref[1] ^ d) * part
        out[:, :, :, :, :half] = low_ref[pl.ds(first, part)]
        out[:, :, :, :, half:] = high_ref[pl.ds(first, part)]


def pack(at, low, high, ys):
    peers, per_peer, boxes, rank, half = low.shape
    shape = jax.ShapeDtypeStruct((peers // ys, per_peer, boxes, rank, 2 * half), jnp.bfloat16)
    return pl.pallas_call(
        pack_kernel,
        in_specs=[SMEM, VMEM, VMEM],
        out_specs=[VMEM] * ys,
        out_shape=[shape] * ys,
        cost_estimate=CHEAP,
    )(at, low, high)


def last_kernel(spec, tail_w, pat_ref, *refs):
    ys, slots = spec["ys"], spec["slots"]
    weights, blocks = refs[:ys], refs[ys : 2 * ys]
    outs, mid = refs[-ys - 1 : -1], refs[-1]
    part, per_peer, boxes, rank, width = weights[0].shape
    half = width // 2

    def level(step, i, source, target):
        for d in range(ys):
            for at, slot in enumerate(slots):
                for g in range(boxes):

                    def term(order):
                        sel = pat_ref[(((d * 2 + step) * part + i) * per_peer + order) * boxes + g]
                        w = weights[d][i, order, g][:, step * half : (step + 1) * half]
                        return product(w, source(d)[i, at, g], source(d ^ (1 + step))[i, at, sel])

                    target(d)[i, at, g] = slot_value(slot, tail_w, per_peer, rank, term)

    def first(i, carry):
        level(0, i, lambda d: blocks[d], lambda d: mid.at[d])
        return carry

    def second(i, carry):
        level(1, i, lambda d: mid.at[d], lambda d: outs[d])
        return carry

    lax.fori_loop(0, part, first, 0)
    lax.fori_loop(0, part, second, 0)


def run_last(tail_w, slots, pattern, weights, blocks, after):
    ys = len(blocks)
    shape = jax.ShapeDtypeStruct(blocks[0].shape, jnp.bfloat16)
    return pl.pallas_call(
        functools.partial(last_kernel, {"ys": ys, "slots": slots}, tail_w),
        in_specs=[SMEM] + [VMEM] * (2 * ys) + [ANY] * len(after),
        out_specs=[VMEM] * ys,
        out_shape=[shape] * ys,
        scratch_shapes=[pltpu.VMEM((ys, *blocks[0].shape), jnp.bfloat16)],
        cost_estimate=CHEAP,
    )(pattern, *weights, *blocks, *after)


def join_kernel(ys, at_ref, *refs):
    out = refs[-1]
    part = refs[0].shape[0]
    for d in range(ys):
        first = (at_ref[1] ^ d) * part
        out[pl.ds(first, part)] = refs[d][...]


def join(at, parts, after):
    ys = len(parts)
    part, *rest = parts[0].shape
    return pl.pallas_call(
        functools.partial(join_kernel, ys),
        in_specs=[SMEM] + [VMEM] * ys + [ANY] * len(after),
        out_specs=VMEM,
        out_shape=jax.ShapeDtypeStruct((ys * part, *rest), jnp.bfloat16),
        cost_estimate=CHEAP,
    )(at, *parts, *after)


def place_kernel(tail_w, slots, me_ref, assign_ref, *refs):
    out_ref = refs[-1]
    peers, per_peer, boxes = refs[0].shape[0], len(slots), refs[0].shape[2]
    local = peers * per_peer
    me = me_ref[0]

    def peer(k, carry):
        for j, (src, at) in enumerate(slots):
            to = assign_ref[k * local + me * per_peer + j] - me * local
            for g in range(boxes):
                value = refs[src][k, at, g]
                if out_ref.shape[-1] < LANES:
                    value = value.astype(jnp.float32)
                    if j:
                        value = pltpu.roll(value, LANES - j * tail_w, 1)
                    value = value[:, :tail_w].astype(jnp.bfloat16)
                out_ref[to, g] = value
        return carry

    lax.fori_loop(0, peers, peer, 0, unroll=2)


def place(tail_w, slots, parts, me, assign, cols, after=()):
    peers, _, boxes, rank, _ = parts[0].shape
    vmem = pl.BlockSpec(memory_space=pltpu.VMEM)
    smem = pl.BlockSpec(memory_space=pltpu.SMEM)
    return pl.pallas_call(
        functools.partial(place_kernel, tail_w, slots),
        in_specs=[smem, smem] + [vmem] * len(parts) + [pl.BlockSpec(memory_space=pl.ANY)] * len(after),
        out_specs=vmem,
        out_shape=jax.ShapeDtypeStruct((peers * len(slots), boxes, rank, cols), jnp.bfloat16),
        cost_estimate=pl.CostEstimate(flops=1, bytes_accessed=1, transcendentals=0),
    )(me, assign, *parts, *after)


def store_kernel(start, *refs):
    piece, out, sems = refs[0], refs[-2], refs[-1]
    boxes, width = piece.shape[:2]
    part = width // sems.shape[1]
    copies = [
        pltpu.make_async_copy(
            piece.at[g, pl.ds(q * part, part)], out.at[g, pl.ds(start + q * part, part)], sems.at[g, q]
        )
        for g in range(boxes)
        for q in range(sems.shape[1])
    ]
    for copy in copies:
        copy.start()
    for copy in copies:
        copy.wait()


def store(piece, start, cols, whole=None):
    boxes, _, rank, local = piece.shape
    held = [] if whole is None else [whole]
    return pl.pallas_call(
        functools.partial(store_kernel, start),
        in_specs=[pl.BlockSpec(memory_space=pltpu.VMEM)] + [pl.BlockSpec(memory_space=pl.ANY)] * len(held),
        out_specs=pl.BlockSpec(memory_space=pl.ANY),
        out_shape=jax.ShapeDtypeStruct((boxes, cols, rank, local), jnp.bfloat16),
        scratch_shapes=[pltpu.SemaphoreType.DMA((boxes, 4 if piece.shape[1] % 4 == 0 else 1))],
        input_output_aliases={1: 0} if held else {},
        cost_estimate=pl.CostEstimate(flops=1, bytes_accessed=1, transcendentals=0),
    )(piece, *held)


def per_device(coeffs, coupling, pattern, assign):
    local, boxes, rank, cols = coeffs.shape
    peers = lax.axis_size("order")
    per_peer = local // peers
    tail_w = cols - 2 * LANES
    order_at = lax.axis_index("order").astype(jnp.int32)
    lat_at = lax.axis_index("lat").astype(jnp.int32)
    ys = lax.axis_size("lat") >> 2
    me = jnp.stack([order_at, lat_at >> 2])

    def six(x):
        return x.reshape(peers, per_peer, boxes, rank, x.shape[-1])

    def level_weights(c, l):
        return six(c[l])

    first = six(coeffs[..., :LANES])
    coeffs, coupling_later, first = lax.optimization_barrier((coeffs, coupling, first))
    first_far = from_partner(first, 1)
    weights = [level_weights(coupling, 0)] + [level_weights(coupling_later, l) for l in range(1, coupling.shape[0])]
    flat_pattern = pattern.reshape(-1)

    after = []

    def level(lev, slots, own, far, spread=0):
        outs = run_level(lev, tail_w, slots, me, flat_pattern, weights[lev], own, far, after, spread)
        after[:] = outs[:1]
        return outs

    def split(groups, tail_at):
        return [[("t", tail_at, 0) if j == TAIL else ("m", 0, j, j) for j in group] for group in groups]

    def own_slots(group):
        return [("t", 0, i) if j == TAIL else ("m", 0, i, j) for i, j in enumerate(group)]

    def places(members):
        arrays, found = [], {}
        for m in members:
            array, offset = done[m]
            if not arrays or arrays[-1] is not array:
                arrays.append(array)
            for i, j in enumerate(groups[m]):
                found[j] = (len(arrays) - 1, offset + i)
        return [found[j] for j in range(per_peer)], arrays

    chunks = list(level(0, split(FIRST, 0), [first], [first_far]))
    second = six(coeffs[..., LANES : 2 * LANES])
    tail = six(coeffs[..., 2 * LANES :]).transpose(0, 2, 3, 1, 4).reshape(peers, boxes, rank, per_peer * tail_w)
    tail = jnp.pad(tail, ((0, 0), (0, 0), (0, 0), (0, LANES - per_peer * tail_w)))[:, None]
    chunks += level(
        0, split(SECOND, 1), [second, tail], [from_partner(second, 1), from_partner(tail, 1)]
    )
    groups = FIRST + SECOND
    tail_chunk = [TAIL in group for group in groups].index(True)
    far = [from_partner(chunk, 2) for chunk in chunks]
    packed = pack(me, weights[2], weights[3], ys)
    packed = [packed[0]] + [from_partner(packed[d], 4 * d) for d in range(1, ys)]
    after.append(packed[0])
    by_peer = pattern[2:].reshape(2, ys, -1).transpose(1, 0, 2).reshape(ys, -1)
    choices = [lax.dynamic_index_in_dim(by_peer, me[1] ^ d, 0, keepdims=False) for d in range(ys)]
    choices = jnp.concatenate([choices[0]] + [from_partner(choices[d], 4 * d) for d in range(1, ys)])

    where = [own_slots(group) for group in groups]
    done = [None] * len(chunks)
    whole = None
    for k, step in ORDER:
        if (k, step) == EARLY:
            early = place(tail_w, *places(range(len(FIRST))), me, assign, LANES)
            whole = store(early.transpose(1, 3, 2, 0), 0, cols)
            after.append(whole)
        after += [done[w][0] for w in WAITS.get((k, step), ())]
        for w in BEHIND.get((k, step), ()):
            after += chunks[w][1:] if isinstance(chunks[w], list) else [far[w]]
        if step == 1:
            outs = level(1, [where[k]], [chunks[k]], [far[k]], ys)
        elif step == 2:
            outs = run_last(tail_w, where[k], choices, packed, chunks[k], after)
        else:
            outs = [join(me, chunks[k], after)]
            done[k] = (lax.all_to_all(outs[0], "order", split_axis=0, concat_axis=0, tiled=True), 0)
        after[:] = outs[:1]
        chunks[k] = [outs[0]] + [from_partner(out, 4 * (d + 1)) for d, out in enumerate(outs[1:])]
    array, offset = done[tail_chunk]
    tail_slot = offset + groups[tail_chunk].index(TAIL)
    ends = place(tail_w, [(0, tail_slot)] * per_peer, [array], me, assign, tail_w, after)
    whole = store(ends.transpose(1, 3, 2, 0), 2 * LANES, cols, whole)
    late = place(tail_w, *places(range(len(FIRST), len(groups))), me, assign, LANES, [whole])
    whole = store(late.transpose(1, 3, 2, 0), LANES, cols, whole)
    return whole.transpose(3, 0, 2, 1)


def solution(mesh):
    return jax.shard_map(
        per_device,
        mesh=mesh,
        in_specs=(
            P("order", "lat", None, None),
            P(None, "order", "lat", None, None),
            P(None, "order", "lat"),
            P(),
        ),
        out_specs=P("order", "lat", None, None),
        check_vma=False,
    )
```
